512 devices in a mesh: ctx: 32 (over x_lo, z), tp: 8 (over y, core), rep: 2 (over x_hi).
Axes of the slice: x: 4 (x_hi: 2, x_lo: 2; x = x_hi * 2 + x_lo), y: 4, z: 16, core: 2. Of those that a mesh axis runs over, the one named last changes fastest.
Arguments:
- queries: bfloat16 [1024, 16384], P(('rep', 'ctx'), 'tp'), parts along dimension 0, may hold values from -8 to 8
- cache_k: bfloat16 [32768, 1024], P(('rep', 'ctx'), 'tp'), parts along dimension 0, may hold values from -8 to 8
- cached_values: bfloat16 [32768, 1024], P(('rep', 'ctx'), 'tp'), parts along dimension 0, may hold values from -6 to 6
- new_token_keys: bfloat16 [1024, 1024], P(('rep', 'ctx'), 'tp'), parts along dimension 0, may hold values from -6 to 6
- new_token_values: bfloat16 [1024, 1024], P(('rep', 'ctx'), 'tp'), parts along dimension 0, may hold values from -6 to 6
- cache_lengths: int32 [64], P(('rep', 'ctx')), parts along dimension 0, may hold values from 2 to 512, as said below
- start_pos: int32 [2], P('rep'), parts along dimension 0, may hold values from 64 to 16384
- out_weight: bfloat16 [16384, 16384], P('tp', 'ctx'), may hold values from -0.046875 to 0.046875
Outputs:
- mixed: float32 [1024, 16384], P(('rep', 'tp'), 'ctx'), parts along dimension 0
The draws below stay inside these ranges and needn't reach their ends.
There are 2 independent parts, one for each index of `rep`. The reference program is written for one: setup_inputs(seed, part) draws one part's arguments, and reference() takes and returns one part's arrays. A program takes and returns all parts, laid end to end along the dimension named above; an argument that names none is the same for every part. Nothing has to cross between parts.
Inputs may be any that keep to these rules, and one draw needn't show every extreme that they name: `cache_lengths`: some cache block is full, with 512 filled slots.
All inputs are finite; a program needn't handle non-finite values.
Results may differ from the reference program's by a relative error of at most 0.014.
Values may be sent and summed in bfloat16 or wider, within the bound.
No kernel may reach another device: no remote copies, remote signals or barrier semaphores. Data moves between devices by JAX's collectives and lax.ppermute only.
A program may use at most 64 MiB of HBM per device.

```python
import jax
import jax.numpy as jnp
from jax import lax

D = 16384
QUERY_HEADS = 128
KEY_VALUE_HEADS = 8
HEAD_SIZE = 128
QDEV = 16
CDEV = 512
NEW_TOKENS = 512
CACHE_SLOTS = 16384
N_CTX = 32


def draw_queries(key, part):
    key = jax.random.fold_in(key, 1)
    seq_tokens = QDEV * N_CTX
    value_rows = jnp.clip(jax.random.normal(key, (seq_tokens, QUERY_HEADS, HEAD_SIZE), jnp.float32), -6.0, 6.0)
    return value_rows.reshape(seq_tokens, QUERY_HEADS * HEAD_SIZE).astype(jnp.bfloat16)


def draw_cache_k(key, part):
    key = jax.random.fold_in(key, 2)
    every_slot = CDEV * N_CTX
    value_rows = jnp.clip(jax.random.normal(key, (every_slot, KEY_VALUE_HEADS, HEAD_SIZE), jnp.float32), -6.0, 6.0)
    return value_rows.reshape(every_slot, KEY_VALUE_HEADS * HEAD_SIZE).astype(jnp.bfloat16)


def draw_cache_lengths(key, part):
    key = jax.random.fold_in(key, 3)
    lengths = jax.random.randint(key, (N_CTX,), 2, CDEV // 2 + 1)
    full_index = jax.random.randint(jax.random.fold_in(key, 4), (), 0, N_CTX)
    return jnp.where(jnp.arange(N_CTX) == full_index, CDEV, lengths).astype(jnp.int32)


def levels(own_key, shape, pieces, least, largest):
    level, own = 1.0, jax.random.fold_in(own_key, 6)
    for position, parts in pieces:
        draws = jnp.exp(jax.random.uniform(jax.random.fold_in(own, position), (parts,), jnp.float32, least / len(pieces), largest / len(pieces)))
        level = level * jnp.repeat(draws, shape[position] // parts).reshape([-1 if axis == position else 1 for axis in range(len(shape))])
    return level


def centred(own_key, extent, spread, bound, pieces=(), held_as=jnp.bfloat16):
    level = levels(own_key, extent, pieces, -0.22, 0.18) if pieces else 1.0
    array = jax.random.normal(own_key, extent, jnp.float32) * spread * level
    return jnp.minimum(jnp.maximum(array, -bound), bound).astype(held_as)


def setup_inputs(seed: int = 0, part: int = 0) -> dict:
    key_of = jax.random.split(jax.random.key(seed), 9)
    own_keys = jax.random.split(jax.random.fold_in(key_of[8], part), 9)
    return {
        "queries": draw_queries(jax.random.fold_in(jax.random.fold_in(key_of[8], part), 71), part),
        "cache_k": draw_cache_k(jax.random.fold_in(jax.random.fold_in(key_of[8], part), 71), part),
        "cached_values": centred(own_keys[2], (CACHE_SLOTS, KEY_VALUE_HEADS * HEAD_SIZE), 1.0, 6.0, ((0, 32), (1, 8))),
        "new_token_keys": centred(own_keys[3], (NEW_TOKENS, KEY_VALUE_HEADS * HEAD_SIZE), 1.0, 6.0, ((0, 32), (1, 8))),
        "new_token_values": centred(own_keys[4], (NEW_TOKENS, KEY_VALUE_HEADS * HEAD_SIZE), 1.0, 6.0, ((0, 32), (1, 8))),
        "cache_lengths": draw_cache_lengths(jax.random.fold_in(jax.random.fold_in(key_of[8], part), 71), part),
        "start_pos": jax.random.randint(own_keys[6], (1,), 2 * N_CTX, CDEV * N_CTX + 1).astype(jnp.int32),
        "out_weight": centred(key_of[7], (QUERY_HEADS * HEAD_SIZE, D), (QUERY_HEADS * HEAD_SIZE) ** -0.5, 0.046875, ((0, 8), (1, 32))),
    }


far_away = 1073741824
very_low = -1.0e30


def reference(queries, cache_k, cached_values, new_token_keys, new_token_values, cache_lengths, start_pos, out_weight):
    begin_pos = start_pos[0]
    seq_tokens = QDEV * N_CTX
    slot_ids = jnp.arange(CDEV, dtype=jnp.int32)
    device_ids = jnp.arange(N_CTX, dtype=jnp.int32)
    slot_pos = slot_ids[None, :] * N_CTX + device_ids[:, None]
    live_slot = (slot_ids[None, :] < cache_lengths[:, None]) & (slot_pos < begin_pos)
    cache_pos = jnp.where(live_slot, slot_pos, far_away)
    query_pos = begin_pos + jnp.arange(seq_tokens, dtype=jnp.int32)
    stretch_pos = query_pos.reshape(N_CTX, QDEV)
    block_pos = jnp.concatenate([cache_pos, stretch_pos], 1)
    visible = block_pos[None, :, :] <= query_pos[:, None, None]
    head_cluster = QUERY_HEADS // KEY_VALUE_HEADS
    factor = HEAD_SIZE ** -0.5

    def one_head(head_index):
        query_head = lax.dynamic_slice_in_dim(queries, head_index * HEAD_SIZE, HEAD_SIZE, 1)
        kv_index = head_index // head_cluster
        cache_key_head = lax.dynamic_slice_in_dim(cache_k, kv_index * HEAD_SIZE, HEAD_SIZE, 1).reshape(N_CTX, CDEV, HEAD_SIZE)
        stretch_key_head = lax.dynamic_slice_in_dim(new_token_keys, kv_index * HEAD_SIZE, HEAD_SIZE, 1).reshape(N_CTX, QDEV, HEAD_SIZE)
        cache_val_head = lax.dynamic_slice_in_dim(cached_values, kv_index * HEAD_SIZE, HEAD_SIZE, 1).reshape(N_CTX, CDEV, HEAD_SIZE)
        stretch_val_head = lax.dynamic_slice_in_dim(new_token_values, kv_index * HEAD_SIZE, HEAD_SIZE, 1).reshape(N_CTX, QDEV, HEAD_SIZE)
        key_head = jnp.concatenate([cache_key_head, stretch_key_head], 1).astype(jnp.float32)
        value_head = jnp.concatenate([cache_val_head, stretch_val_head], 1).astype(jnp.float32)
        scores = jnp.einsum("td,cjd->tcj", query_head.astype(jnp.float32), key_head) * factor
        scores = jnp.where(visible, scores, very_low)
        block_max = jnp.max(scores, axis=2)
        weights = jnp.where(visible, jnp.exp(scores - block_max[..., None]), 0.0)
        block_norm = jnp.maximum(jnp.sum(weights, axis=2), 1.0)
        block_out = jnp.einsum("tcj,cjd->tcd", weights.astype(jnp.bfloat16).astype(jnp.float32), value_head)
        block_value = (block_out / block_norm[..., None]).astype(jnp.bfloat16).astype(jnp.float32)
        block_level = block_max + jnp.log(block_norm)
        top_level = jnp.max(block_level, axis=1, keepdims=True)
        scale_each = jnp.exp(block_level - top_level)
        joined = jnp.sum(block_value * scale_each[..., None], axis=1) / jnp.sum(scale_each, axis=1)[:, None]
        return joined.astype(jnp.bfloat16)

    heads = lax.map(one_head, jnp.arange(QUERY_HEADS, dtype=jnp.int32))
    attended = heads.transpose(1, 0, 2).reshape(seq_tokens, QUERY_HEADS * HEAD_SIZE)
    return jnp.dot(attended, out_weight, preferred_element_type=jnp.float32)
```

```python
import functools

import jax
import jax.numpy as jnp
import numpy as np
from jax import lax
from jax.experimental import pallas as pl
from jax.experimental.pallas import tpu as pltpu
from jax.sharding import PartitionSpec as P

HEAD_SIZE = 128
RING = 16
LANES = 128
very_low = -1e30
far_away = 1073741824
FACTOR = float(HEAD_SIZE ** (-0.5) * np.log2(np.e))
VMEM_LIMIT = 48 * 1024 * 1024


SHARERS = (0, 1, RING, RING + 1)
ACROSS = [(c, c ^ RING) for c in range(2 * RING)]
EIGHTS = [[x * RING + p + 2 * i for i in range(RING // 2)] for x in range(2) for p in range(2)]
RINGS = [[x * RING + z for z in range(RING)] for x in range(2)]
WIRE = jnp.float16
QUERY_SCALE = 4096.0
ROW_TOP = 13


def vmem_specs(count):
    return [pl.BlockSpec(memory_space=pltpu.VMEM)] * count


PARAMS = pltpu.CompilerParams(vmem_limit_bytes=VMEM_LIMIT)


def pack_kernel(length_ref, k_ref, nk_ref, v_ref, nv_ref, o_ref, sems):
    cached, rows = k_ref.shape[0], nk_ref.shape[0]
    copies, start = [], 0
    for i, ref in enumerate((k_ref, nk_ref, v_ref, nv_ref)):
        size = ref.shape[0]
        copies.append(
            pltpu.make_async_copy(ref, o_ref.at[pl.ds(start, size)], sems.at[i])
        )
        copies[-1].start()
        start += size
    row = lax.broadcasted_iota(jnp.int32, (16, LANES), 0)
    filled = length_ref[0]
    digit = jnp.where(row < 8, filled // 16, filled % 16)
    o_ref[2 * (cached + rows) :] = digit.astype(jnp.float32).astype(jnp.bfloat16)
    for copy in copies:
        copy.wait()


def pack(length, k, nk, v, nv):
    total = 2 * (k.shape[0] + nk.shape[0]) + 16
    return pl.pallas_call(
        pack_kernel,
        out_shape=jax.ShapeDtypeStruct((total, LANES), jnp.bfloat16),
        in_specs=[pl.BlockSpec(memory_space=pltpu.SMEM)]
        + [pl.BlockSpec(memory_space=pltpu.HBM)] * 4,
        out_specs=pl.BlockSpec(memory_space=pltpu.VMEM),
        scratch_shapes=[pltpu.SemaphoreType.DMA((4,))],
        compiler_params=PARAMS,
        name="pack",
    )(length, k, nk, v, nv)


def attend_kernel(heads, rows, cached, sizes, place_ref, q_ref, *refs):
    kv_refs = refs[: len(SHARERS)]
    o_ref, k_all, v_all = refs[len(SHARERS) :]
    begin, me = place_ref[0], place_ref[1]
    span = cached + rows
    fresh = len(SHARERS) * rows
    cycle = 2 * RING
    keys = k_all.shape[0]

    k_all[cached:] = jnp.zeros((keys - cached, HEAD_SIZE), jnp.bfloat16)
    v_all[cached:, :HEAD_SIZE] = jnp.zeros((keys - cached, HEAD_SIZE), jnp.bfloat16)
    v_all[:, HEAD_SIZE:] = jnp.ones((keys, HEAD_SIZE), jnp.bfloat16)
    lane = lax.broadcasted_iota(jnp.int32, (1, LANES), 1)
    new_pos = jnp.full((1, LANES), far_away, jnp.int32)
    starts, ends = [], []
    end = fresh
    for i, (sharer, ref) in enumerate(zip(SHARERS, kv_refs)):
        index = jnp.bitwise_xor(me, sharer)
        at = slice(i * rows, (i + 1) * rows)
        k_all[at] = ref[cached:span]
        v_all[at, :HEAD_SIZE] = ref[span + cached : 2 * span]
        new_pos = jnp.where(
            (lane >= i * rows) & (lane < (i + 1) * rows), index * rows + lane - i * rows, new_pos
        )
        digits = ref[2 * span :].astype(jnp.float32)
        filled = jnp.max(digits[:1] * 16 + digits[8:9]).astype(jnp.int32)
        live = jnp.minimum(filled, (begin - index + cycle - 1) // cycle)
        to = pl.ds(pl.multiple_of(end, 16), cached)
        k_all[to, :] = ref[:cached]
        v_all[to, :HEAD_SIZE] = ref[span : span + cached]
        starts.append(end)
        ends.append(end + live)
        end = end + (live + 15) // 16 * 16

    token = lax.broadcasted_iota(jnp.int32, (heads * rows, LANES), 0) % rows
    lanes = lax.broadcasted_iota(jnp.int32, (rows, LANES), 1)
    parity, x = me % 2, me // RING

    def run(size):
        slot = lax.broadcasted_iota(jnp.int32, (1, size), 1)
        seen = functools.reduce(
            jnp.logical_or, [(slot >= a) & (slot < b) for a, b in zip(starts, ends)]
        )
        bias = jnp.where(seen, 0.0, very_low)

        def one(chunk):
            at = pl.ds(pl.multiple_of(chunk * rows, rows), rows)
            query = jnp.concatenate(
                [q_ref[at, h * HEAD_SIZE : (h + 1) * HEAD_SIZE] for h in range(heads)], axis=0
            )
            scores = lax.dot_general(
                query, k_all[:size], (((1,), (1,)), ((), ())), preferred_element_type=jnp.float32
            )
            old = scores[:, LANES:] + bias[:, LANES:]
            first = scores[:, :LANES]
            owner = x * RING + parity + 2 * chunk
            visible = new_pos <= token + owner * rows
            mixed = jnp.where(lane < fresh, jnp.where(visible, first, very_low), first + bias[:, :LANES])
            top = jnp.maximum(
                jnp.max(old, axis=1, keepdims=True), jnp.max(mixed, axis=1, keepdims=True)
            )
            weights = jnp.concatenate(
                [
                    jnp.exp2((mixed - top) * FACTOR).astype(jnp.bfloat16),
                    jnp.exp2((old - top) * FACTOR).astype(jnp.bfloat16),
                ],
                axis=1,
            )
            both = jnp.dot(weights, v_all[:size], preferred_element_type=jnp.float32)
            norm = both[:, HEAD_SIZE:]
            value = both[:, :HEAD_SIZE] / norm
            level = top * FACTOR + jnp.log2(norm)
            packed = jnp.zeros((rows, LANES), jnp.float32)
            for h in range(heads):
                part = slice(h * rows, (h + 1) * rows)
                o_ref[at, h * HEAD_SIZE : (h + 1) * HEAD_SIZE] = value[part].astype(jnp.bfloat16)
                packed = jnp.where(lanes == h, level[part], packed)
            o_ref[at, heads * HEAD_SIZE :] = pack_level(packed)

        @pl.loop(0, RING // 4)
        def _(pair):
            one(2 * pair)
            one(2 * pair + 1)

    below = 0
    for size in sizes:
        pl.when((end > below) & (end <= size))(functools.partial(run, size))
        below = size


def attend(position, gathered, blocks, rows):
    count, width = gathered.shape
    heads = width // HEAD_SIZE
    cached = (blocks[0].shape[0] - 16) // 2 - rows
    most = -(-len(blocks) * (cached + rows) // LANES) * LANES
    sizes = tuple(-(-most * i // 4 // LANES) * LANES for i in (1, 2, 3, 4))
    return pl.pallas_call(
        functools.partial(attend_kernel, heads, rows, cached, sizes),
        out_shape=jax.ShapeDtypeStruct((count, width + LANES), jnp.bfloat16),
        in_specs=[pl.BlockSpec(memory_space=pltpu.SMEM)] + vmem_specs(1 + len(blocks)),
        out_specs=pl.BlockSpec(memory_space=pltpu.VMEM),
        scratch_shapes=[
            pltpu.VMEM((most, HEAD_SIZE), jnp.bfloat16),
            pltpu.VMEM((most, 2 * HEAD_SIZE), jnp.bfloat16),
        ],
        compiler_params=PARAMS,
        cost_estimate=pl.CostEstimate(
            flops=6 * count * heads * most * HEAD_SIZE,
            bytes_accessed=4 << 20,
            transcendentals=count * heads * most,
        ),
        name="attend",
    )(position, gathered, *blocks)


def pack_level(level):
    high = level.astype(jnp.bfloat16).astype(jnp.float32)
    middle = (level - high).astype(jnp.bfloat16).astype(jnp.float32)
    low = (level - high - middle).astype(jnp.bfloat16).astype(jnp.float32)
    spread = high + pltpu.roll(middle, 32, 1) + pltpu.roll(low, 64, 1)
    return spread.astype(jnp.bfloat16)


def unpack_level(spread):
    spread = spread.astype(jnp.float32)
    return spread + pltpu.roll(spread, 96, 1) + pltpu.roll(spread, 64, 1)


def merge_kernel(rows, heads, parts_ref, o_ref, value_ref):
    lane = lax.broadcasted_iota(jnp.int32, (rows, LANES), 1)
    parts = [slice(i * rows, (i + 1) * rows) for i in range(parts_ref.shape[0] // rows)]
    levels = [unpack_level(parts_ref[at, heads * HEAD_SIZE :]) for at in parts]
    top = functools.reduce(jnp.maximum, levels)
    weights = [jnp.exp2(level - top) for level in levels]
    total = 1 / sum(weights)
    scales = [weight * total for weight in weights]
    largest = jnp.zeros((rows, HEAD_SIZE), jnp.float32)
    for h in range(heads):
        span = slice(h * HEAD_SIZE, (h + 1) * HEAD_SIZE)
        value = sum(
            parts_ref[at, span].astype(jnp.float32) * scale[:, h : h + 1]
            for at, scale in zip(parts, scales)
        )
        value_ref[:, span] = value
        largest = jnp.maximum(largest, jnp.abs(value))
    largest = jnp.max(largest, axis=1, keepdims=True)
    power = jnp.floor(jnp.log2(jnp.maximum(largest, 1e-30)))
    o_ref[:, : heads * HEAD_SIZE] = value_ref[...] * jnp.exp2(ROW_TOP - power)
    o_ref[:, heads * HEAD_SIZE :] = jnp.where(lane >= 0, power, 0.0)


def merge(parts, rows):
    width = parts.shape[1]
    heads = width // HEAD_SIZE - 1
    return pl.pallas_call(
        functools.partial(merge_kernel, rows, heads),
        out_shape=jax.ShapeDtypeStruct((rows, width), jnp.float32),
        in_specs=vmem_specs(1),
        out_specs=pl.BlockSpec(memory_space=pltpu.VMEM),
        scratch_shapes=[pltpu.VMEM((rows, heads * HEAD_SIZE), jnp.float32)],
        compiler_params=PARAMS,
        name="merge",
    )(parts)


def attention(
    queries,
    cache_k,
    cached_values,
    new_token_keys,
    new_token_values,
    cache_lengths,
    start_pos,
):
    me = lax.axis_index("ctx")
    rows = queries.shape[0]
    mine = pack(cache_lengths, cache_k, new_token_keys, cached_values, new_token_values)
    blocks = [mine] + [
        lax.ppermute(mine, "ctx", [(c, c ^ sharer) for c in range(2 * RING)])
        for sharer in SHARERS[1:]
    ]
    gathered = lax.all_gather(
        (queries.astype(jnp.float32) * QUERY_SCALE).astype(WIRE),
        "ctx", axis=0, tiled=True, axis_index_groups=EIGHTS,
    )
    gathered = (gathered.astype(jnp.float32) * (1 / QUERY_SCALE)).astype(jnp.bfloat16)
    position = jnp.stack([start_pos[0], me]).astype(jnp.int32)
    parts = attend(position, gathered, blocks, rows)
    parts = lax.all_to_all(parts, "ctx", 0, 0, tiled=True, axis_index_groups=EIGHTS)
    return merge(parts, rows), gathered


def attended_rows(scaled):
    rows = scaled[:, :-LANES].astype(jnp.float32) * jnp.exp2(
        scaled[:, -LANES : 1 - LANES].astype(jnp.float32) - ROW_TOP
    )
    return rows.astype(jnp.bfloat16)


def project_kernel(place_ref, rows_ref, weight_ref, their_ref, o_ref):
    x = place_ref[0]
    height = rows_ref.shape[0]
    for ref, column in ((weight_ref, x), (their_ref, 1 - x)):
        at = pl.ds(pl.multiple_of(column * height, height), height)
        o_ref[at, :] = jnp.dot(
            rows_ref[...], ref[...], preferred_element_type=jnp.float32
        ).astype(jnp.bfloat16)


def project(x, rows, weight, theirs):
    height, depth = rows.shape
    width = weight.shape[1]
    return pl.pallas_call(
        project_kernel,
        out_shape=jax.ShapeDtypeStruct((2 * height, width), jnp.bfloat16),
        in_specs=[pl.BlockSpec(memory_space=pltpu.SMEM)] + vmem_specs(3),
        out_specs=pl.BlockSpec(memory_space=pltpu.VMEM),
        compiler_params=PARAMS,
        cost_estimate=pl.CostEstimate(
            flops=4 * height * depth * width, bytes_accessed=6 << 20, transcendentals=0
        ),
        name="project",
    )(x, rows, weight, theirs)


def local(*arguments):
    out_weight = arguments[-1]
    scaled, first = attention(*arguments[:-1])
    their_weight, _ = lax.optimization_barrier((out_weight, first))
    their_weight = lax.ppermute(their_weight, "ctx", ACROSS)
    scaled = lax.all_gather(
        scaled.astype(WIRE), "ctx", axis=0, tiled=True, axis_index_groups=RINGS
    )
    x = (lax.axis_index("ctx") // RING).astype(jnp.int32).reshape(1)
    terms = project(x, attended_rows(scaled), out_weight, their_weight)
    terms = lax.all_to_all(terms.reshape(8, -1, terms.shape[1]), "tp", 0, 0, tiled=True)
    block = jnp.sum(terms.astype(jnp.float32), axis=0)
    home = [
        ((x * RING + z) * 8 + j, ((j // 4) * RING + z) * 8 + 4 * x + j % 4)
        for x in range(2)
        for z in range(RING)
        for j in range(8)
    ]
    return lax.ppermute(block, ("ctx", "tp"), home)


def solution(mesh):
    placed = (
        P(("rep", "ctx"), "tp"),
        P(("rep", "ctx"), "tp"),
        P(("rep", "ctx"), "tp"),
        P(("rep", "ctx"), "tp"),
        P(("rep", "ctx"), "tp"),
        P(("rep", "ctx")),
        P("rep"),
        P("tp", "ctx"),
    )
    return jax.shard_map(
        local, mesh=mesh, in_specs=placed, out_specs=P(("rep", "tp"), "ctx"), check_vma=False
    )
```

```python
import functools

import jax
import jax.numpy as jnp
import numpy as np
from jax import lax
from jax.experimental import pallas as pl
from jax.experimental.pallas import tpu as pltpu
from jax.sharding import PartitionSpec as P

HEAD_SIZE = 128
RING = 16
LANES = 128
very_low = -1e30
far_away = 1073741824
FACTOR = float(HEAD_SIZE ** (-0.5) * np.log2(np.e))
VMEM_LIMIT = 48 * 1024 * 1024


SHARED = ((0, 0), (1, 0), (0, 1), (1, 1))
ACROSS = [(c, c ^ RING) for c in range(2 * RING)]
EIGHTS = [[x * RING + p + 2 * i for i in range(RING // 2)] for x in range(2) for p in range(2)]
PAIRS_OF_CORES = [
    [(x * RING + z) * 8 + 2 * y + core for x in range(2) for core in range(2)]
    for z in range(RING)
    for y in range(4)
]
RINGS = [[x * RING + z for z in range(RING)] for x in range(2)]
WIRE = jnp.float16
QUERY_SCALE = 4096.0
ROW_TOP = 13


def vmem_specs(count):
    return [pl.BlockSpec(memory_space=pltpu.VMEM)] * count


PARAMS = pltpu.CompilerParams(vmem_limit_bytes=VMEM_LIMIT)


def pack_kernel(length_ref, k_ref, nk_ref, v_ref, nv_ref, o_ref, sems):
    cached, rows = k_ref.shape[0], nk_ref.shape[0]
    total = 2 * (cached + rows)
    size = total + 16
    copies, start = [], 0
    for i, ref in enumerate((k_ref, nk_ref, v_ref, nv_ref)):
        count = ref.shape[0]
        copies.append(pltpu.make_async_copy(ref, o_ref.at[pl.ds(start, count)], sems.at[i]))
        copies[-1].start()
        start += count
    row = lax.broadcasted_iota(jnp.int32, (16, LANES), 0)
    filled = length_ref[0]
    digit = jnp.where(row < 8, filled // 16, filled % 16)
    o_ref[total:size] = digit.astype(jnp.float32).astype(jnp.bfloat16)
    for copy in copies:
        copy.wait()


def pack(length, k, nk, v, nv):
    total = 2 * (k.shape[0] + nk.shape[0]) + 16
    return pl.pallas_call(
        pack_kernel,
        out_shape=jax.ShapeDtypeStruct((total, LANES), jnp.bfloat16),
        in_specs=[pl.BlockSpec(memory_space=pltpu.SMEM)]
        + [pl.BlockSpec(memory_space=pltpu.HBM)] * 4,
        out_specs=pl.BlockSpec(memory_space=pltpu.VMEM),
        scratch_shapes=[pltpu.SemaphoreType.DMA((4,))],
        compiler_params=pltpu.CompilerParams(vmem_limit_bytes=60 * 1024 * 1024),
        name="pack",
    )(length, k, nk, v, nv)


def attend_kernel(heads, rows, cached, sizes, place_ref, q_ref, *refs):
    kv_refs = refs[: len(SHARED)]
    o_ref, k_all, v_all = refs[len(SHARED) :]
    begin, me = place_ref[0], place_ref[1]
    span = cached + rows
    fresh = len(SHARED) * rows
    cycle = 2 * RING
    keys = k_all.shape[0]

    k_all[cached:] = jnp.zeros((keys - cached, HEAD_SIZE), jnp.bfloat16)
    v_all[cached:, :HEAD_SIZE] = jnp.zeros((keys - cached, HEAD_SIZE), jnp.bfloat16)
    v_all[:, HEAD_SIZE:] = jnp.ones((keys, HEAD_SIZE), jnp.bfloat16)
    lane = lax.broadcasted_iota(jnp.int32, (1, LANES), 1)
    new_pos = jnp.full((1, LANES), far_away, jnp.int32)
    starts, ends = [], []
    end = fresh
    x, z = me // RING, me % RING
    for i, ((dx, dz), ref) in enumerate(zip(SHARED, kv_refs)):
        index = lax.rem(x + dx, 2) * RING + lax.rem(z + dz, RING)
        at = slice(i * rows, (i + 1) * rows)
        k_all[at] = ref[cached:span]
        v_all[at, :HEAD_SIZE] = ref[span + cached : 2 * span]
        new_pos = jnp.where(
            (lane >= i * rows) & (lane < (i + 1) * rows), index * rows + lane - i * rows, new_pos
        )
        digits = ref[2 * span :].astype(jnp.float32)
        filled = jnp.max(digits[:1] * 16 + digits[8:9]).astype(jnp.int32)
        live = jnp.minimum(filled, (begin - index + cycle - 1) // cycle)
        to = pl.ds(pl.multiple_of(end, 16), cached)
        k_all[to, :] = ref[:cached]
        v_all[to, :HEAD_SIZE] = ref[span : span + cached]
        starts.append(end)
        ends.append(end + live)
        end = end + (live + 15) // 16 * 16

    token = lax.broadcasted_iota(jnp.int32, (heads * rows, LANES), 0) % rows
    lanes = lax.broadcasted_iota(jnp.int32, (rows, LANES), 1)
    parity = me % 2

    def run(size):
        slot = lax.broadcasted_iota(jnp.int32, (1, size), 1)
        seen = functools.reduce(
            jnp.logical_or, [(slot >= a) & (slot < b) for a, b in zip(starts, ends)]
        )
        bias = jnp.where(seen, 0.0, very_low)

        def one(chunk):
            at = pl.ds(pl.multiple_of(chunk * rows, rows), rows)
            query = jnp.concatenate(
                [q_ref[at, h * HEAD_SIZE : (h + 1) * HEAD_SIZE] for h in range(heads)], axis=0
            )
            scores = lax.dot_general(
                query, k_all[:size], (((1,), (1,)), ((), ())), preferred_element_type=jnp.float32
            )
            old = scores[:, LANES:] + bias[:, LANES:]
            first = scores[:, :LANES]
            owner = x * RING + parity + 2 * chunk
            visible = new_pos <= token + owner * rows
            mixed = jnp.where(lane < fresh, jnp.where(visible, first, very_low), first + bias[:, :LANES])
            top = jnp.maximum(
                jnp.max(old, axis=1, keepdims=True), jnp.max(mixed, axis=1, keepdims=True)
            )
            weights = jnp.concatenate(
                [
                    jnp.exp2((mixed - top) * FACTOR).astype(jnp.bfloat16),
                    jnp.exp2((old - top) * FACTOR).astype(jnp.bfloat16),
                ],
                axis=1,
            )
            both = jnp.dot(weights, v_all[:size], preferred_element_type=jnp.float32)
            norm = both[:, HEAD_SIZE:]
            value = both[:, :HEAD_SIZE] / norm
            level = top * FACTOR + jnp.log2(norm)
            packed = jnp.zeros((rows, LANES), jnp.float32)
            for h in range(heads):
                part = slice(h * rows, (h + 1) * rows)
                o_ref[at, h * HEAD_SIZE : (h + 1) * HEAD_SIZE] = value[part].astype(jnp.bfloat16)
                packed = jnp.where(lanes == h, level[part], packed)
            o_ref[at, heads * HEAD_SIZE :] = pack_level(packed)

        @pl.loop(0, RING // 4)
        def _(pair):
            one(2 * pair)
            one(2 * pair + 1)

    below = 0
    for size in sizes:
        pl.when((end > below) & (end <= size))(functools.partial(run, size))
        below = size


def attend(position, gathered, blocks, rows):
    count, width = gathered.shape
    heads = width // HEAD_SIZE
    cached = (blocks[0].shape[0] - 16) // 2 - rows
    most = -(-len(SHARED) * (cached + rows) // LANES) * LANES
    sizes = tuple(-(-most * i // 4 // LANES) * LANES for i in (1, 2, 3, 4))
    return pl.pallas_call(
        functools.partial(attend_kernel, heads, rows, cached, sizes),
        out_shape=jax.ShapeDtypeStruct((count, width + LANES), jnp.bfloat16),
        in_specs=[pl.BlockSpec(memory_space=pltpu.SMEM)] + vmem_specs(1 + len(blocks)),
        out_specs=pl.BlockSpec(memory_space=pltpu.VMEM),
        scratch_shapes=[
            pltpu.VMEM((most, HEAD_SIZE), jnp.bfloat16),
            pltpu.VMEM((most, 2 * HEAD_SIZE), jnp.bfloat16),
        ],
        compiler_params=PARAMS,
        cost_estimate=pl.CostEstimate(
            flops=6 * count * heads * most * HEAD_SIZE,
            bytes_accessed=4 << 20,
            transcendentals=count * heads * most,
        ),
        name="attend",
    )(position, gathered, *blocks)


def pack_level(level):
    high = level.astype(jnp.bfloat16).astype(jnp.float32)
    middle = (level - high).astype(jnp.bfloat16).astype(jnp.float32)
    low = (level - high - middle).astype(jnp.bfloat16).astype(jnp.float32)
    spread = high + pltpu.roll(middle, 32, 1) + pltpu.roll(low, 64, 1)
    return spread.astype(jnp.bfloat16)


def unpack_level(spread):
    spread = spread.astype(jnp.float32)
    return spread + pltpu.roll(spread, 96, 1) + pltpu.roll(spread, 64, 1)


def merge_kernel(rows, heads, parts_ref, o_ref, value_ref):
    lane = lax.broadcasted_iota(jnp.int32, (rows, LANES), 1)
    parts = [slice(i * rows, (i + 1) * rows) for i in range(parts_ref.shape[0] // rows)]
    levels = [unpack_level(parts_ref[at, heads * HEAD_SIZE :]) for at in parts]
    top = functools.reduce(jnp.maximum, levels)
    weights = [jnp.exp2(level - top) for level in levels]
    total = 1 / sum(weights)
    scales = [weight * total for weight in weights]
    largest = jnp.zeros((rows, HEAD_SIZE), jnp.float32)
    for h in range(heads):
        span = slice(h * HEAD_SIZE, (h + 1) * HEAD_SIZE)
        value = sum(
            parts_ref[at, span].astype(jnp.float32) * scale[:, h : h + 1]
            for at, scale in zip(parts, scales)
        )
        value_ref[:, span] = value
        largest = jnp.maximum(largest, jnp.abs(value))
    largest = jnp.max(largest, axis=1, keepdims=True)
    power = jnp.floor(jnp.log2(jnp.maximum(largest, 1e-30)))
    o_ref[:, : heads * HEAD_SIZE] = value_ref[...] * jnp.exp2(ROW_TOP - power)
    o_ref[:, heads * HEAD_SIZE :] = jnp.where(lane >= 0, power, 0.0)


def merge(parts, rows):
    width = parts.shape[1]
    heads = width // HEAD_SIZE - 1
    return pl.pallas_call(
        functools.partial(merge_kernel, rows, heads),
        out_shape=jax.ShapeDtypeStruct((rows, width), jnp.float32),
        in_specs=vmem_specs(1),
        out_specs=pl.BlockSpec(memory_space=pltpu.VMEM),
        scratch_shapes=[pltpu.VMEM((rows, heads * HEAD_SIZE), jnp.float32)],
        compiler_params=PARAMS,
        name="merge",
    )(parts)


def attention(
    queries,
    cache_k,
    cached_values,
    new_token_keys,
    new_token_values,
    cache_lengths,
    start_pos,
):
    me = lax.axis_index("ctx")
    rows = queries.shape[0]
    mine = pack(cache_lengths, cache_k, new_token_keys, cached_values, new_token_values)
    blocks = [mine] + [
        lax.ppermute(
            mine,
            "ctx",
            [
                ((x + dx) % 2 * RING + (z + dz) % RING, x * RING + z)
                for x in range(2)
                for z in range(RING)
            ],
        )
        for dx, dz in SHARED[1:]
    ]
    gathered = lax.all_gather(
        (queries.astype(jnp.float32) * QUERY_SCALE).astype(WIRE),
        "ctx", axis=0, tiled=True, axis_index_groups=EIGHTS,
    )
    gathered = (gathered.astype(jnp.float32) * (1 / QUERY_SCALE)).astype(jnp.bfloat16)
    position = jnp.stack([start_pos[0], me]).astype(jnp.int32)
    parts = attend(position, gathered, blocks, rows)
    parts = lax.all_to_all(parts, "ctx", 0, 0, tiled=True, axis_index_groups=EIGHTS)
    return merge(parts, rows), gathered


def attended_rows(scaled):
    rows = scaled[:, :-LANES].astype(jnp.float32) * jnp.exp2(
        scaled[:, -LANES : 1 - LANES].astype(jnp.float32) - ROW_TOP
    )
    return rows.astype(jnp.bfloat16)


def project_kernel(place_ref, rows_ref, weight_ref, their_ref, o_ref):
    x = place_ref[0]
    height = rows_ref.shape[0]
    chunk = height // 4
    for ref, column in ((weight_ref, x), (their_ref, 1 - x)):
        product = jnp.dot(
            rows_ref[...], ref[...], preferred_element_type=jnp.float32
        ).astype(jnp.bfloat16)
        for i in range(4):
            to = column * height + ((i % 2) * 2 + i // 2) * chunk
            o_ref[pl.ds(pl.multiple_of(to, chunk), chunk), :] = product[
                i * chunk : (i + 1) * chunk
            ]


def project(x, rows, weight, theirs):
    height, depth = rows.shape
    width = weight.shape[1]
    return pl.pallas_call(
        project_kernel,
        out_shape=jax.ShapeDtypeStruct((2 * height, width), jnp.bfloat16),
        in_specs=[pl.BlockSpec(memory_space=pltpu.SMEM)] + vmem_specs(3),
        out_specs=pl.BlockSpec(memory_space=pltpu.VMEM),
        compiler_params=PARAMS,
        cost_estimate=pl.CostEstimate(
            flops=4 * height * depth * width, bytes_accessed=6 << 20, transcendentals=0
        ),
        name="project",
    )(x, rows, weight, theirs)


def local(*arguments):
    out_weight = arguments[-1]
    scaled, first = attention(*arguments[:-1])
    their_weight, _ = lax.optimization_barrier((out_weight, first))
    their_weight = lax.ppermute(their_weight, "ctx", ACROSS)
    scaled = lax.all_gather(
        scaled.astype(WIRE), "ctx", axis=0, tiled=True, axis_index_groups=RINGS
    )
    rows = attended_rows(scaled)
    x = (lax.axis_index("ctx") // RING).astype(jnp.int32)
    terms = project(x.reshape(1), rows, out_weight, their_weight)
    terms = lax.all_to_all(
        terms, ("ctx", "tp"), 0, 0, tiled=True, axis_index_groups=PAIRS_OF_CORES
    )
    terms = terms.reshape(2, 2, -1, terms.shape[1]).astype(jnp.float32)
    terms = jnp.sum(terms, axis=1).astype(jnp.bfloat16)
    terms = terms.reshape(-1, terms.shape[2])
    terms = lax.all_to_all(terms, "tp", 0, 0, tiled=True, axis_index_groups=[[0, 2, 4, 6], [1, 3, 5, 7]])
    return jnp.sum(terms.reshape(4, -1, terms.shape[1]).astype(jnp.float32), axis=0)


def solution(mesh):
    placed = (
        P(("rep", "ctx"), "tp"),
        P(("rep", "ctx"), "tp"),
        P(("rep", "ctx"), "tp"),
        P(("rep", "ctx"), "tp"),
        P(("rep", "ctx"), "tp"),
        P(("rep", "ctx")),
        P("rep"),
        P("tp", "ctx"),
    )
    return jax.shard_map(
        local, mesh=mesh, in_specs=placed, out_specs=P(("rep", "tp"), "ctx"), check_vma=False
    )
```

```python
import functools

import jax
import jax.numpy as jnp
import numpy as np
from jax import lax
from jax.experimental import pallas as pl
from jax.experimental.pallas import tpu as pltpu
from jax.sharding import PartitionSpec as P

HEAD_SIZE = 128
RING = 16
LANES = 128
very_low = -1e30
far_away = 1073741824
FACTOR = float(HEAD_SIZE ** (-0.5) * np.log2(np.e))
VMEM_LIMIT = 32 * 1024 * 1024


SHARED = ((0, 0), (1, 0), (0, 1), (1, 1))
ACROSS = [(c, c ^ RING) for c in range(2 * RING)]
EIGHTS = [[x * RING + p + 2 * i for i in range(RING // 2)] for x in range(2) for p in range(2)]
PAIRS_OF_CORES = [
    [(x * RING + z) * 8 + 2 * y + core for x in range(2) for core in range(2)]
    for z in range(RING)
    for y in range(4)
]
RINGS = [[x * RING + z for z in range(RING)] for x in range(2)]
WIRE = jnp.float16
POWER_LANE = 96
QUERY_SCALE = 4096.0
ROW_TOP = 13


def vmem_specs(count):
    return [pl.BlockSpec(memory_space=pltpu.VMEM)] * count


PARAMS = pltpu.CompilerParams(vmem_limit_bytes=VMEM_LIMIT)


def pack_kernel(length_ref, k_ref, nk_ref, v_ref, nv_ref, o_ref, sems):
    cached, rows = k_ref.shape[0], nk_ref.shape[0]
    total = 2 * (cached + rows)
    size = total + 16
    copies, start = [], 0
    for i, ref in enumerate((k_ref, nk_ref, v_ref, nv_ref)):
        count = ref.shape[0]
        copies.append(pltpu.make_async_copy(ref, o_ref.at[pl.ds(start, count)], sems.at[i]))
        copies[-1].start()
        start += count
    row = lax.broadcasted_iota(jnp.int32, (16, LANES), 0)
    filled = length_ref[0]
    digit = jnp.where(row < 8, filled // 16, filled % 16)
    o_ref[total:size] = digit.astype(jnp.float32).astype(jnp.bfloat16)
    for copy in copies:
        copy.wait()


def pack(length, k, nk, v, nv):
    total = 2 * (k.shape[0] + nk.shape[0]) + 16
    return pl.pallas_call(
        pack_kernel,
        out_shape=jax.ShapeDtypeStruct((total, LANES), jnp.bfloat16),
        in_specs=[pl.BlockSpec(memory_space=pltpu.SMEM)]
        + [pl.BlockSpec(memory_space=pltpu.HBM)] * 4,
        out_specs=pl.BlockSpec(memory_space=pltpu.VMEM),
        scratch_shapes=[pltpu.SemaphoreType.DMA((4,))],
        compiler_params=pltpu.CompilerParams(vmem_limit_bytes=60 * 1024 * 1024),
        name="pack",
    )(length, k, nk, v, nv)


def attend_kernel(heads, rows, cached, sizes, place_ref, q_ref, *refs):
    kv_refs = refs[: len(SHARED)]
    o_ref, k_all, v_all = refs[len(SHARED) :]
    begin, me = place_ref[0], place_ref[1]
    span = cached + rows
    fresh = len(SHARED) * rows
    cycle = 2 * RING
    keys = k_all.shape[0]

    k_all[cached:] = jnp.zeros((keys - cached, HEAD_SIZE), jnp.bfloat16)
    v_all[cached:, :HEAD_SIZE] = jnp.zeros((keys - cached, HEAD_SIZE), jnp.bfloat16)
    v_all[:, HEAD_SIZE:] = jnp.ones((keys, HEAD_SIZE), jnp.bfloat16)
    lane = lax.broadcasted_iota(jnp.int32, (1, LANES), 1)
    new_pos = jnp.full((1, LANES), far_away, jnp.int32)
    row = lax.broadcasted_iota(jnp.int32, (cached, HEAD_SIZE), 0)
    starts, ends, live_values = [], [], []
    end = fresh
    x, z = me // RING, me % RING
    for i, ((dx, dz), ref) in enumerate(zip(SHARED, kv_refs)):
        index = lax.rem(x + dx, 2) * RING + lax.rem(z + dz, RING)
        at = slice(i * rows, (i + 1) * rows)
        k_all[at] = ref[cached:span]
        v_all[at, :HEAD_SIZE] = ref[span + cached : 2 * span]
        new_pos = jnp.where(
            (lane >= i * rows) & (lane < (i + 1) * rows), index * rows + lane - i * rows, new_pos
        )
        digits = ref[2 * span :].astype(jnp.float32)
        filled = jnp.max(digits[:1] * 16 + digits[8:9]).astype(jnp.int32)
        live = jnp.minimum(filled, (begin - index + cycle - 1) // cycle)
        to = pl.ds(pl.multiple_of(end, 16), cached)
        k_all[to, :] = ref[:cached]
        v_all[to, :HEAD_SIZE] = ref[span : span + cached]
        values = jnp.abs(ref[span : span + cached].astype(jnp.float32))
        live_values.append(jnp.where(row < live, values, 0.0))
        live_values.append(jnp.abs(ref[span + cached : 2 * span].astype(jnp.float32)))
        starts.append(end)
        ends.append(end + live)
        end = end + (live + 15) // 16 * 16

    largest = functools.reduce(
        jnp.maximum, [jnp.max(part, axis=0, keepdims=True) for part in live_values]
    )
    largest = jnp.max(largest, axis=1, keepdims=True)
    power = jnp.ceil(jnp.log2(jnp.maximum(largest, 1e-30)))

    token = lax.broadcasted_iota(jnp.int32, (heads * rows, LANES), 0) % rows
    lanes = lax.broadcasted_iota(jnp.int32, (rows, LANES), 1)
    parity = me % 2

    def run(size):
        slot = lax.broadcasted_iota(jnp.int32, (1, size), 1)
        seen = functools.reduce(
            jnp.logical_or, [(slot >= a) & (slot < b) for a, b in zip(starts, ends)]
        )
        bias = jnp.where(seen, 0.0, very_low)

        def one(chunk):
            at = pl.ds(pl.multiple_of(chunk * rows, rows), rows)
            query = jnp.concatenate(
                [q_ref[at, h * HEAD_SIZE : (h + 1) * HEAD_SIZE] for h in range(heads)], axis=0
            )
            scores = lax.dot_general(
                query, k_all[:size], (((1,), (1,)), ((), ())), preferred_element_type=jnp.float32
            )
            old = scores[:, LANES:] + bias[:, LANES:]
            first = scores[:, :LANES]
            owner = x * RING + parity + 2 * chunk
            visible = new_pos <= token + owner * rows
            mixed = jnp.where(lane < fresh, jnp.where(visible, first, very_low), first + bias[:, :LANES])
            top = jnp.maximum(
                jnp.max(old, axis=1, keepdims=True), jnp.max(mixed, axis=1, keepdims=True)
            )
            weights = jnp.concatenate(
                [
                    jnp.exp2((mixed - top) * FACTOR).astype(jnp.bfloat16),
                    jnp.exp2((old - top) * FACTOR).astype(jnp.bfloat16),
                ],
                axis=1,
            )
            both = jnp.dot(weights, v_all[:size], preferred_element_type=jnp.float32)
            norm = both[:, HEAD_SIZE:]
            value = both[:, :HEAD_SIZE] / norm
            level = top * FACTOR + jnp.log2(norm)
            packed = jnp.zeros((rows, LANES), jnp.float32)
            for h in range(heads):
                part = slice(h * rows, (h + 1) * rows)
                o_ref[at, h * HEAD_SIZE : (h + 1) * HEAD_SIZE] = value[part].astype(jnp.bfloat16)
                packed = jnp.where(lanes == h, level[part], packed)
            o_ref[at, heads * HEAD_SIZE :] = jnp.where(
                lanes == POWER_LANE, power, pack_level(packed).astype(jnp.float32)
            ).astype(jnp.bfloat16)

        @pl.loop(0, RING // 4)
        def _(pair):
            one(2 * pair)
            one(2 * pair + 1)

    below = 0
    for size in sizes:
        pl.when((end > below) & (end <= size))(functools.partial(run, size))
        below = size


def attend(position, gathered, blocks, rows):
    count, width = gathered.shape
    heads = width // HEAD_SIZE
    cached = (blocks[0].shape[0] - 16) // 2 - rows
    most = -(-len(SHARED) * (cached + rows) // LANES) * LANES
    sizes = tuple(-(-most * i // (8 * LANES)) * LANES for i in range(1, 9))
    return pl.pallas_call(
        functools.partial(attend_kernel, heads, rows, cached, sizes),
        out_shape=jax.ShapeDtypeStruct((count, width + LANES), jnp.bfloat16),
        in_specs=[pl.BlockSpec(memory_space=pltpu.SMEM)] + vmem_specs(1 + len(blocks)),
        out_specs=pl.BlockSpec(memory_space=pltpu.VMEM),
        scratch_shapes=[
            pltpu.VMEM((most, HEAD_SIZE), jnp.bfloat16),
            pltpu.VMEM((most, 2 * HEAD_SIZE), jnp.bfloat16),
        ],
        compiler_params=PARAMS,
        cost_estimate=pl.CostEstimate(
            flops=6 * count * heads * most * HEAD_SIZE,
            bytes_accessed=4 << 20,
            transcendentals=count * heads * most,
        ),
        name="attend",
    )(position, gathered, *blocks)


def pack_level(level):
    high = level.astype(jnp.bfloat16).astype(jnp.float32)
    middle = (level - high).astype(jnp.bfloat16).astype(jnp.float32)
    low = (level - high - middle).astype(jnp.bfloat16).astype(jnp.float32)
    spread = high + pltpu.roll(middle, 32, 1) + pltpu.roll(low, 64, 1)
    return spread.astype(jnp.bfloat16)


def unpack_level(spread):
    spread = spread.astype(jnp.float32)
    return spread + pltpu.roll(spread, 96, 1) + pltpu.roll(spread, 64, 1)


def merge_kernel(rows, heads, parts_ref, o_ref, power_ref):
    parts = [slice(i * rows, (i + 1) * rows) for i in range(parts_ref.shape[0] // rows)]
    tails = [parts_ref[at, heads * HEAD_SIZE :] for at in parts]
    levels = [unpack_level(tail) for tail in tails]
    power = functools.reduce(
        jnp.maximum,
        [tail.astype(jnp.float32)[:, POWER_LANE : POWER_LANE + 1] for tail in tails],
    )
    top = functools.reduce(jnp.maximum, levels)
    weights = [jnp.exp2(level - top) for level in levels]
    total = jnp.exp2(ROW_TOP - power) / sum(weights)
    scales = [weight * total for weight in weights]
    for h in range(heads):
        span = slice(h * HEAD_SIZE, (h + 1) * HEAD_SIZE)
        o_ref[:, span] = sum(
            parts_ref[at, span].astype(jnp.float32) * scale[:, h : h + 1]
            for at, scale in zip(parts, scales)
        )
    power_ref[...] = jnp.broadcast_to(power, power_ref.shape)


def merge(parts, rows):
    width = parts.shape[1]
    heads = width // HEAD_SIZE - 1
    return pl.pallas_call(
        functools.partial(merge_kernel, rows, heads),
        out_shape=[
            jax.ShapeDtypeStruct((rows, heads * HEAD_SIZE), jnp.float32),
            jax.ShapeDtypeStruct((rows, LANES), jnp.float32),
        ],
        in_specs=vmem_specs(1),
        out_specs=vmem_specs(2),
        compiler_params=pltpu.CompilerParams(vmem_limit_bytes=16 * 1024 * 1024),
        name="merge",
    )(parts)


def attention(
    queries,
    cache_k,
    cached_values,
    new_token_keys,
    new_token_values,
    cache_lengths,
    start_pos,
):
    me = lax.axis_index("ctx")
    rows = queries.shape[0]
    mine = pack(cache_lengths, cache_k, new_token_keys, cached_values, new_token_values)
    blocks = [mine] + [
        lax.ppermute(
            mine,
            "ctx",
            [
                ((x + dx) % 2 * RING + (z + dz) % RING, x * RING + z)
                for x in range(2)
                for z in range(RING)
            ],
        )
        for dx, dz in SHARED[1:]
    ]
    gathered = lax.all_gather(
        (queries.astype(jnp.float32) * QUERY_SCALE).astype(WIRE),
        "ctx", axis=0, tiled=True, axis_index_groups=EIGHTS,
    )
    gathered = (gathered.astype(jnp.float32) * (1 / QUERY_SCALE)).astype(jnp.bfloat16)
    position = jnp.stack([start_pos[0], me]).astype(jnp.int32)
    parts = attend(position, gathered, blocks, rows)
    parts = lax.all_to_all(parts, "ctx", 0, 0, tiled=True, axis_index_groups=EIGHTS)
    return merge(parts, rows), gathered


def project_kernel(place_ref, power_ref, rows_ref, weight_ref, their_ref, o_ref):
    x = place_ref[0]
    height = rows_ref.shape[0]
    chunk = height // 4
    scale = jnp.exp2(power_ref[:1, :1] - ROW_TOP)
    for ref, column in ((weight_ref, x), (their_ref, 1 - x)):
        product = jnp.dot(rows_ref[...], ref[...], preferred_element_type=jnp.float32)
        product = (product * scale).astype(jnp.bfloat16)
        for i in range(4):
            to = column * height + ((i % 2) * 2 + i // 2) * chunk
            o_ref[pl.ds(pl.multiple_of(to, chunk), chunk), :] = product[
                i * chunk : (i + 1) * chunk
            ]


def project(x, power, rows, weight, theirs):
    height, depth = rows.shape
    width = weight.shape[1]
    return pl.pallas_call(
        project_kernel,
        out_shape=jax.ShapeDtypeStruct((2 * height, width), jnp.bfloat16),
        in_specs=[pl.BlockSpec(memory_space=pltpu.SMEM)] + vmem_specs(4),
        out_specs=pl.BlockSpec(memory_space=pltpu.VMEM),
        compiler_params=PARAMS,
        cost_estimate=pl.CostEstimate(
            flops=4 * height * depth * width, bytes_accessed=6 << 20, transcendentals=0
        ),
        name="project",
    )(x, power, rows, weight, theirs)


def local(*arguments):
    out_weight = arguments[-1]
    (scaled, power), first = attention(*arguments[:-1])
    their_weight, _ = lax.optimization_barrier((out_weight, first))
    their_weight = lax.ppermute(their_weight, "ctx", ACROSS)
    scaled = lax.all_gather(
        scaled.astype(WIRE), "ctx", axis=0, tiled=True, axis_index_groups=RINGS
    )
    x = (lax.axis_index("ctx") // RING).astype(jnp.int32)
    terms = project(
        x.reshape(1), power, scaled.astype(jnp.bfloat16), out_weight, their_weight
    )
    terms = lax.all_to_all(
        terms, ("ctx", "tp"), 0, 0, tiled=True, axis_index_groups=PAIRS_OF_CORES
    )
    terms = terms.reshape(2, 2, -1, terms.shape[1]).astype(jnp.float32)
    terms = jnp.sum(terms, axis=1).astype(jnp.bfloat16)
    terms = terms.reshape(-1, terms.shape[2])
    terms = lax.all_to_all(terms, "tp", 0, 0, tiled=True, axis_index_groups=[[0, 2, 4, 6], [1, 3, 5, 7]])
    return jnp.sum(terms.reshape(4, -1, terms.shape[1]).astype(jnp.float32), axis=0)


def solution(mesh):
    placed = (
        P(("rep", "ctx"), "tp"),
        P(("rep", "ctx"), "tp"),
        P(("rep", "ctx"), "tp"),
        P(("rep", "ctx"), "tp"),
        P(("rep", "ctx"), "tp"),
        P(("rep", "ctx")),
        P("rep"),
        P("tp", "ctx"),
    )
    return jax.shard_map(
        local, mesh=mesh, in_specs=placed, out_specs=P(("rep", "tp"), "ctx"), check_vma=False
    )
```
